128 devices in a mesh: people: 32 (over y, z, core), markers: 4 (over x).
Axes of the slice: x: 4, y: 4, z: 4, core: 2. Of those that a mesh axis runs over, the one named last changes fastest.
Arguments:
- genotypes: float32 [262144, 1024], P('people', 'markers'), may hold values from -120 to 120, as said below
- sketch: float32 [40, 1024], P(None, 'markers'), may hold values from -6 to 6
Outputs:
- basis: float32 [40, 262144], P(None, 'people')
- loadings: float32 [40, 1024], P(None, 'markers')
The draws below stay inside these ranges and needn't reach their ends.
Inputs may be any that keep to these rules, and one draw needn't show every extreme that they name: `genotypes`: real values of order one; marker columns and individuals have differing scales.
All inputs are finite; a program needn't handle non-finite values.
Results may differ from the reference program's by a relative error of at most 0.00025.
Values sent between devices are 32-bit elements; how exact they have to be, the bound alone decides.
A program may use at most 64 MiB of HBM per device.

```python
import math
import jax
import jax.numpy as jnp
from jax import lax

M = 1024
K = 40
ITERS = 5
PEOPLE = 262144


def draw_genotypes(key, part):
    key = jax.random.fold_in(key, 11)
    noise_key, column_key, person_key, rank_key = jax.random.split(key, 4)
    noise = jnp.clip(jax.random.normal(noise_key, (PEOPLE, M), jnp.float32), -5.0, 5.0)
    person_scale = jnp.exp(jax.random.uniform(person_key, (PEOPLE, 1), jnp.float32, math.log(0.5), math.log(2.0)))
    bulk_scale = jnp.exp(jax.random.uniform(column_key, (1, M), jnp.float32, math.log(0.2), math.log(2.0)))
    marker_rank = jax.random.permutation(rank_key, M).astype(jnp.float32)[None, :]
    leading_scale = 4.0 * jnp.exp(math.log(0.982) * marker_rank)
    column_scale = jnp.maximum(bulk_scale, leading_scale)
    ramp_rows = jnp.exp(math.log(3.0) * jnp.arange(PEOPLE, dtype=jnp.float32) / PEOPLE)[:, None]
    return noise * column_scale * person_scale * ramp_rows


def steps_of(key, shape, pieces, low, largest):
    def one(position, shards_of):
        draws = jax.random.uniform(jax.random.fold_in(jax.random.fold_in(key, 6), position), (shards_of,), jnp.float32, low / len(pieces), largest / len(pieces))
        return jnp.repeat(jnp.exp(draws), shape[position] // shards_of).reshape((-1,) + (1,) * (len(shape) - position - 1))

    level = one(*pieces[0])
    for cut in pieces[1:]:
        level = level * one(*cut)
    return level


def normal_values(stream_key, dims, scale, limit, cuts=(), kind=jnp.bfloat16):
    gain = steps_of(stream_key, dims, cuts, -0.22, 0.18) if cuts else 1.0
    array = jax.random.normal(stream_key, dims, jnp.float32) * scale * gain
    return jnp.minimum(jnp.maximum(array, -limit), limit).astype(kind)


def setup_inputs(seed: int = 0) -> dict:
    key_of = jax.random.split(jax.random.key(seed), 3)
    return {
        "genotypes": draw_genotypes(jax.random.fold_in(key_of[2], 71), 0),
        "sketch": normal_values(key_of[1], (K, M), 1.0, 6.0, ((1, 4),), jnp.float32),
    }


def reference(genotypes, sketch):
    high = lax.Precision.HIGHEST
    current = sketch
    basis_t = None
    for turn_index in range(ITERS):
        sketch_rows = jnp.dot(current, genotypes.T, precision=high)
        gram_total = jnp.dot(sketch_rows, sketch_rows.T, precision=high)
        lower_factor = jnp.linalg.cholesky(gram_total)
        basis_t = jax.scipy.linalg.solve_triangular(lower_factor, sketch_rows, lower=True)
        current = jnp.dot(basis_t, genotypes, precision=high)
    norm_scale = math.sqrt(PEOPLE)
    return (basis_t * norm_scale, current / norm_scale)
```

```python
import math

import jax
import jax.numpy as jnp
from jax import lax
from jax.sharding import PartitionSpec as P

ITERS = 5


def contract(left, right, left_dim, right_dim):
    return lax.dot_general(
        left, right, (((left_dim,), (right_dim,)), ((), ())), precision=lax.Precision.HIGHEST
    )


def local(genotypes, sketch):
    norm_scale = math.sqrt(genotypes.shape[0] * lax.axis_size("people"))
    rows = lax.all_to_all(genotypes, "markers", 0, 1, tiled=True)
    current = lax.all_gather(sketch, "markers", axis=1, tiled=True)
    cov = lax.psum(contract(rows, rows, 0, 0), ("people", "markers"))
    basis_t = None
    for turn_index in range(ITERS):
        image = contract(current, cov, 1, 0)
        gram_total = contract(image, current, 1, 1)
        lower_factor = jnp.linalg.cholesky(gram_total)
        if turn_index == ITERS - 1:
            sketch_rows = contract(current, rows, 1, 1)
            basis_t = jax.scipy.linalg.solve_triangular(lower_factor, sketch_rows, lower=True)
        current = jax.scipy.linalg.solve_triangular(lower_factor, image, lower=True)
    basis = lax.all_gather(basis_t * norm_scale, "markers", axis=1, tiled=True)
    mine = lax.axis_index("markers") * genotypes.shape[1]
    return (basis, lax.dynamic_slice_in_dim(current, mine, genotypes.shape[1], 1) / norm_scale)


def solution(mesh):
    placed = (P("people", "markers"), P(None, "markers"))
    return jax.shard_map(
        local,
        mesh=mesh,
        in_specs=placed,
        out_specs=(P(None, "people"), P(None, "markers")),
        check_vma=False,
    )
```

```python
import functools
import math

import jax
import jax.numpy as jnp
from jax import lax
from jax.experimental import pallas as pl
from jax.experimental.pallas import tpu as pltpu
from jax.sharding import PartitionSpec as P

MESH = pl.DeviceIdType.MESH
ITERS = 5
WIDTHS = (32,) * 8
F32, BF16 = jnp.float32, jnp.bfloat16
NT = (((1,), (1,)), ((), ()))


def contract(left, right, left_dim, right_dim):
    return lax.dot_general(
        left, right, (((left_dim,), (right_dim,)), ((), ())), precision=lax.Precision.HIGHEST
    )


def place():
    people, x = lax.axis_index("people"), lax.axis_index("markers")
    return x, people // 8, lax.rem(people // 2, 4), lax.rem(people, 2)


def device(x, y, z, core):
    return {"people": (y * 4 + z) * 2 + core, "markers": x}


def turn(index, step):
    return lax.rem(index + step, 4)


class Copies:
    def __init__(self, send_sem, recv_sem):
        self.send_sem, self.recv_sem, self.count, self.open = send_sem, recv_sem, 0, []

    def exchange(self, src, dst, to, landed):
        slot = self.count
        self.count += 1
        copy = pltpu.make_async_remote_copy(
            src_ref=src, dst_ref=dst, send_sem=self.send_sem.at[slot], recv_sem=self.recv_sem.at[slot],
            device_id=to, device_id_type=MESH)
        copy.start()
        arrival = pltpu.make_async_remote_copy(
            src_ref=landed, dst_ref=landed, send_sem=self.send_sem.at[slot], recv_sem=self.recv_sem.at[slot],
            device_id=to, device_id_type=MESH)
        self.open.append(copy)
        return arrival

    def finish(self):
        for copy in self.open:
            copy.wait_send()
        self.open = []


def reduce_steps(stage, rows, copies, refs, here):
    acc, full, b1, s1, b2, s2, b3, s3, b4 = refs
    x, y, z, core = here
    base, count = rows
    half, part = count // 2, count // 8
    hb = base // 2
    pb = base // 8
    mine = pl.ds(pl.multiple_of(base + core * half, 8), half)
    other = pl.ds(pl.multiple_of(base + (1 - core) * half, 8), half)
    b1s = b1.at[pl.ds(hb, half)]
    got = copies.exchange(acc.at[other], b1s, device(x, y, z, 1 - core), b1s)
    yield
    got.wait_recv()
    s1[pl.ds(hb, half)] = acc[mine] + b1[pl.ds(hb, half)]
    waits = []

    def row_part(index):
        return pl.ds(pl.multiple_of(hb + index * part, 8), part)

    for o in (1, 2, 3):
        waits.append(copies.exchange(
            s1.at[row_part(turn(y, o)), pl.ds(0, 512)], b2.at[0, o - 1, pl.ds(pb, part)],
            device(x, turn(y, o), z, core), b2.at[0, o - 1, pl.ds(pb, part)]))
        waits.append(copies.exchange(
            s1.at[row_part(turn(z, o)), pl.ds(512, 512)], b2.at[1, o - 1, pl.ds(pb, part)],
            device(x, y, turn(z, o), core), b2.at[1, o - 1, pl.ds(pb, part)]))
    yield
    for w in waits:
        w.wait_recv()
    ps = pl.ds(pb, part)
    s2[0, ps] = s1[row_part(y), 0:512] + b2[0, 0, ps] + b2[0, 1, ps] + b2[0, 2, ps]
    s2[1, ps] = s1[row_part(z), 512:1024] + b2[1, 0, ps] + b2[1, 1, ps] + b2[1, 2, ps]
    waits = []

    def lane_part(index):
        return pl.ds(pl.multiple_of(index * 128, 128), 128)

    for o in (1, 2, 3):
        waits.append(copies.exchange(
            s2.at[0, ps, lane_part(turn(z, o))], b3.at[0, o - 1, ps],
            device(x, y, turn(z, o), core), b3.at[0, o - 1, ps]))
        waits.append(copies.exchange(
            s2.at[1, ps, lane_part(turn(y, o))], b3.at[1, o - 1, ps],
            device(x, turn(y, o), z, core), b3.at[1, o - 1, ps]))
    yield
    for w in waits:
        w.wait_recv()
    for h, index in ((0, z), (1, y)):
        s3[h, ps] = s2[h, ps, lane_part(index)] + b3[h, 0, ps] + b3[h, 1, ps] + b3[h, 2, ps]
    waits = []
    b4[x, :, ps] = s3[:, ps]
    for o in (1, 2, 3):
        waits.append(copies.exchange(
            s3.at[:, ps], b4.at[x, :, ps], device(turn(x, o), y, z, core), b4.at[turn(x, 4 - o), :, ps]))
    yield
    for w in waits:
        w.wait_recv()
    total = (b4[0, :, ps] + b4[1, :, ps]) + (b4[2, :, ps] + b4[3, :, ps])

    def final(h, row, lane):
        r = pl.ds(pl.multiple_of(base + core * half + row * part, 8), part)
        if lane is None:
            return r, pl.ds(512 * h, 512)
        return r, pl.ds(pl.multiple_of(512 * h + lane * 128, 128), 128)

    full[final(0, y, z)] = total[0]
    full[final(1, z, y)] = total[1]
    waits = []
    for o in (1, 2, 3):
        at = full.at[final(0, y, z)]
        waits.append(copies.exchange(at, at, device(x, y, turn(z, o), core), full.at[final(0, y, turn(z, 4 - o))]))
        at = full.at[final(1, z, y)]
        waits.append(copies.exchange(at, at, device(x, turn(y, o), z, core), full.at[final(1, z, turn(y, 4 - o))]))
    yield
    for w in waits:
        w.wait_recv()
    waits = []
    for o in (1, 2, 3):
        at = full.at[final(0, y, None)]
        waits.append(copies.exchange(at, at, device(x, turn(y, o), z, core), full.at[final(0, turn(y, 4 - o), None)]))
        at = full.at[final(1, z, None)]
        waits.append(copies.exchange(at, at, device(x, y, turn(z, o), core), full.at[final(1, turn(z, 4 - o), None)]))
    yield
    for w in waits:
        w.wait_recv()
    at = full.at[mine]
    got = copies.exchange(at, at, device(x, y, z, 1 - core), full.at[other])
    yield
    got.wait_recv()


def gather_kernel(a, full_out, rows_out, staged, turned, rx, hi, lo, acc, full, b1, s1, b2, s2, b3, s3, b4,
                  load_sem, out_sem, send_sem, recv_sem):
    here = x, y, z, core = place()
    chunk = a.shape[0] // 4
    loads = []
    for o in (1, 3, 2, 0):
        load = pltpu.make_async_copy(
            a.at[pl.ds(pl.multiple_of(turn(x, o) * chunk, chunk), chunk)], staged.at[o], load_sem.at[o])
        load.start()
        loads.append((o, load))
    barrier = pltpu.get_barrier_semaphore()
    partners = [device(x, y, z, 1 - core)]
    for o in (1, 2, 3):
        partners += [device(turn(x, o), y, z, core), device(x, turn(y, o), z, core), device(x, y, turn(z, o), core)]
    for partner in partners:
        pl.semaphore_signal(barrier, inc=1, device_id=partner, device_id_type=MESH)
    pl.semaphore_wait(barrier, len(partners))

    copies = Copies(send_sem, recv_sem)
    starts = [sum(WIDTHS[:s]) for s in range(len(WIDTHS))]
    arrivals = {}

    def send(s, o):
        r = pl.ds(starts[s], WIDTHS[s])
        arrivals[s, o] = copies.exchange(
            turned.at[o, r], rx.at[x, r], device(turn(x, o), y, z, core), rx.at[turn(x, 4 - o), r])

    def transpose(o, h):
        @pl.loop(0, chunk // 512)
        def _(i):
            at = pl.ds(pl.multiple_of(i * 512, 512), 512)
            block = staged[o, at, 128 * h:128 * h + 128].T
            if o:
                turned[o, 128 * h:128 * h + 128, at] = block
            else:
                rx[x, 128 * h:128 * h + 128, at] = block

    ahead = 2
    for o, load in loads:
        load.wait()
        transpose(o, 0)
        if o:
            for s in range(ahead):
                send(s, o)
    for o in (1, 3, 2, 0):
        transpose(o, 1)

    refs = (acc, full, b1, s1, b2, s2, b3, s3, b4)
    running = []
    outs = []

    def advance():
        for item in list(running):
            try:
                next(item)
            except StopIteration:
                running.remove(item)

    for s, width in enumerate(WIDTHS):
        base, count = 4 * starts[s], 4 * width
        for o in (1, 3, 2):
            arrivals[s, o].wait_recv()
            if s + ahead < len(WIDTHS):
                send(s + ahead, o)
        for m in range(4):
            value = rx[m, starts[s]:starts[s] + width]
            top = value.astype(BF16)
            hi[base + m * width:base + m * width + width] = top
            lo[base + m * width:base + m * width + width] = (value - top.astype(F32)).astype(BF16)
        out = pltpu.make_async_copy(
            rx.at[:, pl.ds(starts[s], width)], rows_out.at[:, pl.ds(starts[s], width)], out_sem.at[s])
        out.start()
        outs.append(out)
        advance()
        lanes = base + count
        new = pl.ds(base, count)
        acc[new] = jnp.zeros((count, 1024), F32)

        @pl.loop(0, chunk // 512)
        def _(i):
            at = pl.ds(pl.multiple_of(i * 512, 512), 512)
            dot = functools.partial(lax.dot_general, dimension_numbers=NT, preferred_element_type=F32)
            acc[new, 0:lanes] += (dot(hi[new, at], hi[0:lanes, at]) + dot(hi[new, at], lo[0:lanes, at])
                                  + dot(lo[new, at], hi[0:lanes, at]))

        advance()
        item = reduce_steps(s, (base, count), copies, refs, here)
        next(item)
        running.append(item)
    while running:
        advance()
    out = pltpu.make_async_copy(full, full_out, out_sem.at[len(WIDTHS)])
    out.start()
    outs.append(out)
    copies.finish()
    for out in outs:
        out.wait()


def gather(genotypes):
    chunk = genotypes.shape[0] // 4
    n = len(WIDTHS)
    slots = n * (3 + 1 + 6 + 6 + 3 + 6 + 6 + 1)
    return pl.pallas_call(
        gather_kernel,
        name="gather",
        out_shape=(jax.ShapeDtypeStruct((1024, 1024), F32), jax.ShapeDtypeStruct((4, 256, chunk), F32)),
        in_specs=[pl.BlockSpec(memory_space=pl.ANY)],
        out_specs=(pl.BlockSpec(memory_space=pl.ANY),) * 2,
        scratch_shapes=[
            pltpu.VMEM((4, chunk, 256), F32),
            pltpu.VMEM((4, 256, chunk), F32),
            pltpu.VMEM((4, 256, chunk), F32),
            pltpu.VMEM((1024, chunk), BF16),
            pltpu.VMEM((1024, chunk), BF16),
            pltpu.VMEM((1024, 1024), F32),
            pltpu.VMEM((1024, 1024), F32),
            pltpu.VMEM((512, 1024), F32),
            pltpu.VMEM((512, 1024), F32),
            pltpu.VMEM((2, 3, 128, 512), F32),
            pltpu.VMEM((2, 128, 512), F32),
            pltpu.VMEM((2, 3, 128, 128), F32),
            pltpu.VMEM((2, 128, 128), F32),
            pltpu.VMEM((4, 2, 128, 128), F32),
            pltpu.SemaphoreType.DMA((4,)),
            pltpu.SemaphoreType.DMA((n + 1,)),
            pltpu.SemaphoreType.DMA((slots,)),
            pltpu.SemaphoreType.DMA((slots,)),
        ],
        compiler_params=pltpu.CompilerParams(collective_id=0, has_side_effects=True, vmem_limit_bytes=60 << 20),
    )(genotypes)


def local(genotypes, sketch):
    norm_scale = math.sqrt(genotypes.shape[0] * lax.axis_size("people"))
    current = lax.all_gather(sketch, "markers", axis=1, tiled=True)
    lower, rows = gather(genotypes)
    rows = rows.reshape(1024, rows.shape[2])
    n, width = len(WIDTHS), WIDTHS[0]
    block = jnp.arange(1024) // (4 * width)
    low = jnp.where(block[:, None] >= block[None, :], lower, 0.0)
    strict = jnp.where(block[:, None] > block[None, :], lower, 0.0)
    cov = low + strict.T
    cov = cov.reshape(n, 4, width, n, 4, width).transpose(1, 0, 2, 4, 3, 5).reshape(1024, 1024)
    basis_t = None
    for turn_index in range(ITERS):
        image = contract(current, cov, 1, 0)
        gram_total = contract(image, current, 1, 1)
        lower_factor = jnp.linalg.cholesky(gram_total)
        if turn_index == ITERS - 1:
            sketch_rows = contract(current, rows, 1, 0)
            basis_t = jax.scipy.linalg.solve_triangular(lower_factor, sketch_rows, lower=True)
        current = jax.scipy.linalg.solve_triangular(lower_factor, image, lower=True)
    basis = lax.all_gather(basis_t * norm_scale, "markers", axis=1, tiled=True)
    mine = lax.axis_index("markers") * genotypes.shape[1]
    return (basis, lax.dynamic_slice_in_dim(current, mine, genotypes.shape[1], 1) / norm_scale)


def solution(mesh):
    placed = (P("people", "markers"), P(None, "markers"))
    return jax.shard_map(
        local,
        mesh=mesh,
        in_specs=placed,
        out_specs=(P(None, "people"), P(None, "markers")),
        check_vma=False,
    )
```

```python
import functools
import math

import jax
import jax.numpy as jnp
from jax import lax
from jax.experimental import pallas as pl
from jax.experimental.pallas import tpu as pltpu
from jax.sharding import PartitionSpec as P

MESH = pl.DeviceIdType.MESH
ITERS = 5
M, K, PAD = 1024, 40, 48
WIDTHS = (32,) * 7 + (16,) * 2
STARTS = tuple(sum(WIDTHS[:s]) for s in range(len(WIDTHS)))
PIECE = 512
F32, BF16 = jnp.float32, jnp.bfloat16
NT = (((1,), (1,)), ((), ()))
NN = (((1,), (0,)), ((), ()))


def place():
    people, x = lax.axis_index("people"), lax.axis_index("markers")
    return x, people // 8, lax.rem(people // 2, 4), lax.rem(people, 2)


def device(x, y, z, core):
    return {"people": (y * 4 + z) * 2 + core, "markers": x}


def turn(index, step):
    return lax.rem(index + step, 4)


def halves(value):
    top = value.astype(BF16)
    return top, (value - top.astype(F32)).astype(BF16)


def product(left, right_top, right_low, dims):
    rows = left.shape[0]
    top, low = halves(left)
    dot = functools.partial(lax.dot_general, dimension_numbers=dims, preferred_element_type=F32)
    both = dot(jnp.concatenate([top, low], axis=0), right_top)
    return both[:rows] + (both[rows:] + dot(top, right_low))


def inverse_factor(work):
    lane = lax.broadcasted_iota(jnp.int32, (8, 128), 1)
    row = lax.broadcasted_iota(jnp.int32, (8, 128), 0)
    tiles = [work[8 * t:8 * t + 8] + jnp.where(lane == row + 8 * t, 1.0, 0.0) for t in range(K // 8)]
    for j in range(K):
        first, r = divmod(j, 8)
        pivot_row = tiles[first][r:r + 1]
        scaled = pivot_row / pivot_row[:, 64 + j:65 + j]
        for t in range(first, K // 8):
            column = jnp.broadcast_to(tiles[t][:, 64 + j:65 + j], (8, 128))
            if t == first:
                column = jnp.where(row > r, column, 0.0)
            tiles[t] = tiles[t] - column * scaled
    for t in range(K // 8):
        pivots = jnp.sum(jnp.where(lane == row + (64 + 8 * t), tiles[t], 0.0), axis=1, keepdims=True)
        tiles[t] = jnp.where(lane < K, tiles[t] / jnp.sqrt(pivots), 0.0)
    tiles += [jnp.zeros((8, 128), F32)] * ((PAD - K) // 8)
    return jnp.concatenate(tiles, axis=0)[:, :PAD]


class Copies:
    def __init__(self, send_sem, recv_sem):
        self.send_sem, self.recv_sem, self.count, self.open = send_sem, recv_sem, 0, []

    def exchange(self, src, dst, to, landed):
        slot = self.count
        self.count += 1
        copy = pltpu.make_async_remote_copy(
            src_ref=src, dst_ref=dst, send_sem=self.send_sem.at[slot], recv_sem=self.recv_sem.at[slot],
            device_id=to, device_id_type=MESH)
        copy.start()
        self.open.append(copy)
        return pltpu.make_async_remote_copy(
            src_ref=landed, dst_ref=landed, send_sem=self.send_sem.at[slot], recv_sem=self.recv_sem.at[slot],
            device_id=to, device_id_type=MESH)

    def finish(self):
        for copy in self.open:
            copy.wait_send()
        self.open = []


def reduce_steps(base, count, copies, refs, here):
    acc, full, b1, s1, b2, s3, b4 = refs
    x, y, z, core = here
    half, part = count // 2, count // 8
    hb, pb = base // 2, base // 8
    mine = pl.ds(pl.multiple_of(base + core * half, 8), half)
    other = pl.ds(pl.multiple_of(base + (1 - core) * half, 8), half)
    h = pl.ds(hb, half)
    p = pl.ds(pb, part)
    plane = [(i, j) for i in range(4) for j in range(4) if i or j]
    got = copies.exchange(acc.at[other], b1.at[h], device(x, y, z, 1 - core), b1.at[h])
    yield
    got.wait_recv()
    s1[h] = acc[mine] + b1[h]

    def cut(row, lane, offset):
        return (pl.ds(pl.multiple_of(offset + row * part, 8), part), pl.ds(pl.multiple_of(lane * 256, 128), 256))

    waits = []
    for n, (i, j) in enumerate(plane):
        waits.append(copies.exchange(
            s1.at[cut(turn(y, i), turn(z, j), hb)], b2.at[n, p],
            device(x, turn(y, i), turn(z, j), core), b2.at[n, p]))
    yield
    for w in waits:
        w.wait_recv()
    total = s1[cut(y, z, hb)]
    for n in range(len(plane)):
        total = total + b2[n, p]
    s3[p] = total
    b4[x, p] = total
    waits = []
    for o in (1, 2, 3):
        waits.append(copies.exchange(
            s3.at[p], b4.at[x, p], device(turn(x, o), y, z, core), b4.at[turn(x, 4 - o), p]))
    yield
    yield
    for w in waits:
        w.wait_recv()
    offset = base + core * half
    at = full.at[cut(y, z, offset)]
    full[cut(y, z, offset)] = (b4[0, p] + b4[1, p]) + (b4[2, p] + b4[3, p])
    waits = []
    for i, j in plane:
        waits.append(copies.exchange(
            at, at, device(x, turn(y, i), turn(z, j), core), full.at[cut(turn(y, 4 - i), turn(z, 4 - j), offset)]))
    yield
    for w in waits:
        w.wait_recv()
    got = copies.exchange(full.at[mine], full.at[mine], device(x, y, z, 1 - core), full.at[other])
    yield
    got.wait_recv()


def kernel(a, sketch, basis, loadings, staged, turned, rx, hi, lo, acc, full, chi, clo, skb, yb, b1, s1, b2, s3, b4,
           natural, load_sem, piece_send, piece_recv, send_sem, recv_sem):
    here = x, y, z, core = place()
    chunk = a.shape[0] // 4
    pieces = chunk // PIECE
    norm_scale = math.sqrt(a.shape[0] * lax.axis_size("people"))
    loads = {}
    for k in range(pieces):
        for o in (1, 3, 2, 0):
            load = pltpu.make_async_copy(
                a.at[pl.ds(pl.multiple_of(turn(x, o) * chunk + k * PIECE, PIECE), PIECE)],
                staged.at[o, pl.ds(k * PIECE, PIECE)], load_sem.at[k * 4 + o])
            load.start()
            loads[k, o] = load
    barrier = pltpu.get_barrier_semaphore()
    partners = [device(x, y, z, 1 - core)]
    partners += [device(turn(x, o), y, z, core) for o in (1, 2, 3)]
    partners += [device(x, turn(y, i), turn(z, j), core) for i in range(4) for j in range(4) if i or j]
    for partner in partners:
        pl.semaphore_signal(barrier, inc=1, device_id=partner, device_id_type=MESH)

    skb[x] = sketch[...]
    yb[:, K:PAD] = jnp.zeros((4, PAD - K, chunk), F32)
    copies = Copies(send_sem, recv_sem)

    def piece(s, k, o, back=False):
        r, at = pl.ds(STARTS[s], WIDTHS[s]), pl.ds(pl.multiple_of(k * PIECE, PIECE), PIECE)
        sems = dict(send_sem=piece_send.at[(s * pieces + k) * 3 + o - 1],
                    recv_sem=piece_recv.at[(s * pieces + k) * 3 + o - 1],
                    device_id=device(turn(x, o), y, z, core), device_id_type=MESH)
        if back:
            landed = rx.at[turn(x, 4 - o), r, at]
            return pltpu.make_async_remote_copy(src_ref=landed, dst_ref=landed, **sems)
        return pltpu.make_async_remote_copy(src_ref=turned.at[o, r, at], dst_ref=rx.at[x, r, at], **sems)

    def transpose(o, k, h):
        at = pl.ds(k * PIECE, PIECE)
        block = staged[o, at, 128 * h:128 * h + 128].T
        if o:
            turned[o, 128 * h:128 * h + 128, at] = block
        else:
            rx[x, 128 * h:128 * h + 128, at] = block

    ahead = 2
    for k in range(pieces):
        for o in (1, 3, 2):
            loads[k, o].wait()
            transpose(o, k, 0)
            if k == 0 and o == 1:
                pl.semaphore_wait(barrier, len(partners))
            if k < ahead:
                piece(0, k, o).start()
    sketch_waits = [
        copies.exchange(sketch, skb.at[x], device(turn(x, o), y, z, core), skb.at[turn(x, 4 - o)]) for o in (1, 2, 3)]
    for k in range(pieces):
        loads[k, 0].wait()
        transpose(0, k, 0)

    refs = (acc, full, b1, s1, b2, s3, b4)
    running = []

    def keep(base, count):
        value = full[base:base + count, 0:base + count]
        block = value[:, base:base + count]
        if count > 4 * WIDTHS[-1] and base + count == M:
            r = lax.broadcasted_iota(jnp.int32, (count, count), 0)
            c = lax.broadcasted_iota(jnp.int32, (count, count), 1)
            block = jnp.where((r < count // 2) & (c >= count // 2), block.T, block)
        chi[base:base + count, base:base + count], clo[base:base + count, base:base + count] = halves(block)
        if base:
            side = value[:, 0:base]
            chi[base:base + count, 0:base], clo[base:base + count, 0:base] = halves(side)
            chi[0:base, base:base + count], clo[0:base, base:base + count] = halves(side.T)

    def stage_sum(s):
        base, count = 4 * STARTS[s], 4 * WIDTHS[s]
        yield from reduce_steps(base, count, copies, refs, here)
        if WIDTHS[s] == 32:
            keep(base, count)

    def advance():
        for item in list(running):
            try:
                next(item)
            except StopIteration:
                running.remove(item)

    dot_nt = functools.partial(lax.dot_general, dimension_numbers=NT, preferred_element_type=F32)
    step = 0
    for s, width in enumerate(WIDTHS):
        base, count = 4 * STARTS[s], 4 * width
        lanes = base + count
        new = pl.ds(base, count)
        acc[new] = jnp.zeros((count, M), F32)
        for first in range(0, pieces, ahead):

            @pl.loop(first, first + ahead)
            def _(k):
                at = pl.ds(pl.multiple_of(k * PIECE, PIECE), PIECE)
                for o in (1, 3, 2):
                    piece(s, k, o, back=True).wait_recv()
                    piece(s, k, o).wait_send()
                    if first + ahead < pieces:
                        piece(s, k + ahead, o).start()
                    elif s + 1 < len(WIDTHS):
                        piece(s + 1, k + ahead - pieces, o).start()
                for m in range(4):
                    r = pl.ds(base + m * width, width)
                    hi[r, at], lo[r, at] = halves(rx[m, STARTS[s]:STARTS[s] + width, at])
                acc[new, 0:lanes] += (dot_nt(hi[new, at], hi[0:lanes, at]) + dot_nt(hi[new, at], lo[0:lanes, at])
                                      + dot_nt(lo[new, at], hi[0:lanes, at]))

            if step < 4:
                for k in range(pieces):
                    transpose(step, k, 1)
            step += 1
            if first + ahead == pieces:
                running.append(stage_sum(s))
            advance()
    for w in sketch_waits:
        w.wait_recv()
    current = jnp.concatenate(
        [skb[m, :, STARTS[s]:STARTS[s] + WIDTHS[s]] for s in range(len(WIDTHS)) for m in range(4)], axis=1)
    current = jnp.concatenate([current, jnp.zeros((PAD - K, M), F32)], axis=0)
    while running:
        advance()
    keep(M - 128, 128)

    def image_of(value):
        return product(value, chi[...], clo[...], NN)

    def gram_of(image, value):
        top, low = halves(value)
        before, after = jnp.zeros((64, M), BF16), jnp.zeros((64 - PAD, M), BF16)
        return product(image, jnp.concatenate([before, top, after], axis=0),
                       jnp.concatenate([before, low, after], axis=0), NT)

    def apply(inverse, value):
        return product(inverse, *halves(value), NN)

    image = image_of(current)
    gram = gram_of(image, current)
    for turn_index in range(ITERS - 2):
        second = image_of(image)
        inverse = inverse_factor(gram)
        current = apply(inverse, image)
        image = apply(inverse, second)
        gram = gram_of(image, current)

    parts = {}
    top, low = halves(image)
    stacked = jnp.concatenate([top, low], axis=0)
    dot_nn = functools.partial(lax.dot_general, dimension_numbers=NN, preferred_element_type=F32)
    for k in range(pieces):
        at = pl.ds(k * PIECE, PIECE)
        both = dot_nn(stacked, hi[:, at])
        yb[x, 0:K, at] = (both[:PAD] + (both[PAD:] + dot_nn(top, lo[:, at])))[:K]
        for o in (1, 3, 2):
            src = yb.at[x, pl.ds(0, K), at]
            parts[k, o] = copies.exchange(
                src, src, device(turn(x, o), y, z, core), yb.at[turn(x, 4 - o), pl.ds(0, K), at])
    second = image_of(image)
    inverse = inverse_factor(gram)
    current = apply(inverse, image)
    image = apply(inverse, second)
    last = inverse_factor(gram_of(image, current))
    current = apply(last, image)[:K] / norm_scale
    for m in range(4):
        natural[m] = jnp.concatenate(
            [current[:, 4 * r + m * w:4 * r + m * w + w] for r, w in zip(STARTS, WIDTHS)], axis=1)
    loadings[...] = natural[x]
    last = apply(last, inverse) * norm_scale
    for o in (0, 1, 3, 2):
        m = turn(x, 4 - o)
        for k in range(pieces):
            if o:
                parts[k, o].wait_recv()
            value = apply(last, yb[m, :, pl.ds(k * PIECE, PIECE)])
            basis[:, pl.ds(pl.multiple_of(m * chunk + k * PIECE, PIECE), PIECE)] = value[:K]
    copies.finish()


def local(genotypes, sketch):
    chunk = genotypes.shape[0] // 4
    n, pieces = len(WIDTHS), chunk // PIECE
    slots = n * (1 + 15 + 3 + 15 + 1) + 3 + 3 * pieces
    vmem = pl.BlockSpec(memory_space=pltpu.VMEM)
    return pl.pallas_call(
        kernel,
        name="subspace_iteration",
        out_shape=(jax.ShapeDtypeStruct((K, genotypes.shape[0]), F32), jax.ShapeDtypeStruct((K, 256), F32)),
        in_specs=[pl.BlockSpec(memory_space=pl.ANY), vmem],
        out_specs=(vmem, vmem),
        scratch_shapes=[
            pltpu.VMEM((4, chunk, 256), F32),
            pltpu.VMEM((4, 256, chunk), F32),
            pltpu.VMEM((4, 256, chunk), F32),
            pltpu.VMEM((M, chunk), BF16),
            pltpu.VMEM((M, chunk), BF16),
            pltpu.VMEM((M, M), F32),
            pltpu.VMEM((M, M), F32),
            pltpu.VMEM((M, M), BF16),
            pltpu.VMEM((M, M), BF16),
            pltpu.VMEM((4, K, 256), F32),
            pltpu.VMEM((4, PAD, chunk), F32),
            pltpu.VMEM((M // 2, M), F32),
            pltpu.VMEM((M // 2, M), F32),
            pltpu.VMEM((15, M // 8, 256), F32),
            pltpu.VMEM((M // 8, 256), F32),
            pltpu.VMEM((4, M // 8, 256), F32),
            pltpu.VMEM((4, K, 256), F32),
            pltpu.SemaphoreType.DMA((4 * pieces,)),
            pltpu.SemaphoreType.DMA((n * pieces * 3,)),
            pltpu.SemaphoreType.DMA((n * pieces * 3,)),
            pltpu.SemaphoreType.DMA((slots,)),
            pltpu.SemaphoreType.DMA((slots,)),
        ],
        compiler_params=pltpu.CompilerParams(collective_id=0, has_side_effects=True, vmem_limit_bytes=62 << 20),
    )(genotypes, sketch)


def solution(mesh):
    placed = (P("people", "markers"), P(None, "markers"))
    return jax.shard_map(
        local,
        mesh=mesh,
        in_specs=placed,
        out_specs=(P(None, "people"), P(None, "markers")),
        check_vma=False,
    )
```

```python
import functools
import math

import jax
import jax.numpy as jnp
from jax import lax
from jax.experimental import pallas as pl
from jax.experimental.pallas import tpu as pltpu
from jax.sharding import PartitionSpec as P

MESH = pl.DeviceIdType.MESH
ITERS = 5
M, K, PAD = 1024, 40, 48
WIDTHS = (128, 32, 32, 16, 16, 16, 16)
PIECES = (512, 512, 512, 1024, 1024, 1024, 512)
STARTS = tuple(sum(WIDTHS[:s]) for s in range(len(WIDTHS)))
PAUSES = ((1, 4, 5, 4, 1),) + ((1, 3, 4, 3, 1),) * 2 + ((1, 2, 3, 2, 1),) * 4
F32, BF16 = jnp.float32, jnp.bfloat16
NT = (((1,), (1,)), ((), ()))
NN = (((1,), (0,)), ((), ()))


def place():
    people, x = lax.axis_index("people"), lax.axis_index("markers")
    return x, people // 8, lax.rem(people // 2, 4), lax.rem(people, 2)


def device(x, y, z, core):
    return {"people": (y * 4 + z) * 2 + core, "markers": x}


def turn(index, step):
    return lax.rem(index + step, 4)


def halves(value):
    top = value.astype(BF16)
    return top, (value - top.astype(F32)).astype(BF16)


def product(left, right_top, right_low, dims):
    rows = left.shape[0]
    top, low = halves(left)
    dot = functools.partial(lax.dot_general, dimension_numbers=dims, preferred_element_type=F32)
    both = dot(jnp.concatenate([top, low], axis=0), right_top)
    return both[:rows] + (both[rows:] + dot(top, right_low))


def inverse_factor(work):
    lane = lax.broadcasted_iota(jnp.int32, (8, 128), 1)
    row = lax.broadcasted_iota(jnp.int32, (8, 128), 0)
    tiles = [work[8 * t:8 * t + 8] + jnp.where(lane == row + 8 * t, 1.0, 0.0) for t in range(K // 8)]
    for j in range(K):
        first, r = divmod(j, 8)
        pivot_row = tiles[first][r:r + 1]
        scaled = pivot_row / pivot_row[:, 64 + j:65 + j]
        for t in range(first, K // 8):
            column = jnp.broadcast_to(tiles[t][:, 64 + j:65 + j], (8, 128))
            if t == first:
                column = jnp.where(row > r, column, 0.0)
            tiles[t] = tiles[t] - column * scaled
    for t in range(K // 8):
        pivots = jnp.sum(jnp.where(lane == row + (64 + 8 * t), tiles[t], 0.0), axis=1, keepdims=True)
        tiles[t] = jnp.where(lane < K, tiles[t] / jnp.sqrt(pivots), 0.0)
    tiles += [jnp.zeros((8, 128), F32)] * ((PAD - K) // 8)
    return jnp.concatenate(tiles, axis=0)[:, :PAD]


class Copies:
    def __init__(self, send_sem, recv_sem):
        self.send_sem, self.recv_sem, self.count, self.open = send_sem, recv_sem, 0, []

    def exchange(self, src, dst, to, landed):
        slot = self.count
        self.count += 1
        copy = pltpu.make_async_remote_copy(
            src_ref=src, dst_ref=dst, send_sem=self.send_sem.at[slot], recv_sem=self.recv_sem.at[slot],
            device_id=to, device_id_type=MESH)
        copy.start()
        self.open.append(copy)
        return pltpu.make_async_remote_copy(
            src_ref=landed, dst_ref=landed, send_sem=self.send_sem.at[slot], recv_sem=self.recv_sem.at[slot],
            device_id=to, device_id_type=MESH)

    def finish(self):
        for copy in self.open:
            copy.wait_send()
        self.open = []


def reduce_steps(base, count, span, pauses, copies, refs, here):
    acc, full, b1, s1, b2, s3, b4 = refs
    x, y, z, core = here
    half, part, wide = count // 2, count // 8, span // 4
    hb, pb = base // 2, base // 8
    lanes = pl.ds(0, span)
    mine = pl.ds(pl.multiple_of(base + core * half, 8), half)
    other = pl.ds(pl.multiple_of(base + (1 - core) * half, 8), half)
    h = pl.ds(hb, half)
    p = (pl.ds(pb, part), pl.ds(0, wide))
    plane = [(i, j) for i in range(4) for j in range(4) if i or j]
    got = copies.exchange(acc.at[other, lanes], b1.at[h, lanes], device(x, y, z, 1 - core), b1.at[h, lanes])
    yield from (None,) * pauses[0]
    got.wait_recv()
    s1[h, lanes] = acc[mine, lanes] + b1[h, lanes]

    def cut(row, lane, offset):
        return (pl.ds(pl.multiple_of(offset + row * part, 8), part), pl.ds(pl.multiple_of(lane * wide, 128), wide))

    waits = []
    for n, (i, j) in enumerate(plane):
        waits.append(copies.exchange(
            s1.at[cut(turn(y, i), turn(z, j), hb)], b2.at[(n,) + p],
            device(x, turn(y, i), turn(z, j), core), b2.at[(n,) + p]))
    yield from (None,) * pauses[1]
    for w in waits:
        w.wait_recv()
    total = s1[cut(y, z, hb)]
    for n in range(len(plane)):
        total = total + b2[(n,) + p]
    s3[p] = total
    b4[(x,) + p] = total
    waits = []
    for o in (2, 1, 3):
        waits.append(copies.exchange(
            s3.at[p], b4.at[(x,) + p], device(turn(x, o), y, z, core), b4.at[(turn(x, 4 - o),) + p]))
    yield from (None,) * pauses[2]
    for w in waits:
        w.wait_recv()
    offset = base + core * half
    at = full.at[cut(y, z, offset)]
    full[cut(y, z, offset)] = (b4[(0,) + p] + b4[(1,) + p]) + (b4[(2,) + p] + b4[(3,) + p])
    waits = []
    for i, j in plane:
        waits.append(copies.exchange(
            at, at, device(x, turn(y, i), turn(z, j), core), full.at[cut(turn(y, 4 - i), turn(z, 4 - j), offset)]))
    yield from (None,) * pauses[3]
    for w in waits:
        w.wait_recv()
    at = full.at[mine, lanes]
    got = copies.exchange(at, at, device(x, y, z, 1 - core), full.at[other, lanes])
    yield from (None,) * pauses[4]
    got.wait_recv()


def kernel(a, sketch, basis, loadings, raw, staged, turned, rx, hi, lo, acc, full, chi, clo, skb, yb, b1, s1, b2, s3,
           b4, natural, start, load_sem, piece_send, piece_recv, send_sem, recv_sem):
    here = x, y, z, core = place()
    chunk = a.shape[0] // 4
    own = pl.ds(pl.multiple_of(x * chunk, chunk), chunk)
    first_half, second_half = pl.ds(0, 128), pl.ds(128, 128)
    own_raw = pltpu.make_async_copy(a.at[own, first_half], raw.at[x], load_sem.at[0])
    own_raw.start()
    barrier = pltpu.get_barrier_semaphore()
    partners = [device(x, y, z, 1 - core)]
    partners += [device(turn(x, o), y, z, core) for o in (1, 2, 3)]
    partners += [device(x, turn(y, i), turn(z, j), core) for i in range(4) for j in range(4) if i or j]
    for partner in partners:
        pl.semaphore_signal(barrier, inc=1, device_id=partner, device_id_type=MESH)
    copies = Copies(send_sem, recv_sem)
    order = [(s, k) for s in range(len(WIDTHS)) for k in range(chunk // PIECES[s])]

    def piece(g, o, back=False):
        s, k = order[g]
        at = pl.ds(k * PIECES[s], PIECES[s])
        sems = dict(send_sem=piece_send.at[g * 3 + o - 1], recv_sem=piece_recv.at[g * 3 + o - 1],
                    device_id=device(turn(x, o), y, z, core), device_id_type=MESH)
        if s == 0:
            src = a.at[pl.ds(pl.multiple_of(turn(x, o) * chunk + k * PIECES[s], PIECES[s]), PIECES[s]), first_half]
            spot = (at,)
            into = raw
        else:
            r = pl.ds(STARTS[s] - 128, WIDTHS[s])
            src = turned.at[o - 1, r, at]
            spot = (r, at)
            into = rx
        if back:
            landed = into.at[(turn(x, 4 - o),) + spot]
            return pltpu.make_async_remote_copy(src_ref=landed, dst_ref=landed, **sems)
        return pltpu.make_async_remote_copy(src_ref=src, dst_ref=into.at[(x,) + spot], **sems)

    ahead = 2
    pl.semaphore_wait(barrier, len(partners))
    for g in range(ahead):
        for o in (1, 3, 2):
            piece(g, o).start()
    skb[x] = sketch[...]
    sketch_waits = [
        copies.exchange(sketch, skb.at[x], device(turn(x, o), y, z, core), skb.at[turn(x, 4 - o)]) for o in (1, 2, 3)]
    loads = {}
    for o in range(4):
        load = pltpu.make_async_copy(
            a.at[pl.ds(pl.multiple_of(turn(x, o) * chunk, chunk), chunk), second_half], staged.at[o], load_sem.at[o + 1])
        load.start()
        loads[o] = load
    yb[:, K:PAD] = jnp.zeros((4, PAD - K, chunk), F32)

    def transpose(o, k):
        at = pl.ds(k * PIECES[0], PIECES[0])
        block = staged[o, at].T
        if o:
            turned[o - 1, :, at] = block
        else:
            rx[x, :, at] = block

    for o in range(4):
        loads[o].wait()
        transpose(o, 0)
    own_raw.wait()

    refs = (acc, full, b1, s1, b2, s3, b4)
    running = []

    def keep(base, count, halved=False):
        value = full[base:base + count, 0:base + count]
        block = value[:, base:base + count]
        if halved:
            r = lax.broadcasted_iota(jnp.int32, (count, count), 0)
            c = lax.broadcasted_iota(jnp.int32, (count, count), 1)
            block = jnp.where((r < count // 2) & (c >= count // 2), block.T, block)
        chi[base:base + count, base:base + count], clo[base:base + count, base:base + count] = halves(block)
        if base:
            side = value[:, 0:base]
            chi[base:base + count, 0:base], clo[base:base + count, 0:base] = halves(side)
            chi[0:base, base:base + count], clo[0:base, base:base + count] = halves(side.T)

    def stage_sum(s):
        base, count = 4 * STARTS[s], 4 * WIDTHS[s]
        yield from reduce_steps(base, count, M if s else count, PAUSES[s], copies, refs, here)
        if WIDTHS[s] > 16:
            keep(base, count)
        elif s % 2 == 0 and base + count < M:
            keep(base - count, 2 * count, True)

    def advance():
        for item in reversed(list(running)):
            try:
                next(item)
            except StopIteration:
                running.remove(item)

    dot_nt = functools.partial(lax.dot_general, dimension_numbers=NT, preferred_element_type=F32)
    unit = jnp.where(lax.broadcasted_iota(jnp.int32, (128, 128), 0) == lax.broadcasted_iota(jnp.int32, (128, 128), 1),
                     1.0, 0.0).astype(BF16)
    for g, (s, k) in enumerate(order):
        width, size = WIDTHS[s], PIECES[s]
        base, count = 4 * STARTS[s], 4 * width
        lanes = base + count
        at = pl.ds(k * size, size)
        new = pl.ds(base, count)
        for o in (1, 3, 2):
            piece(g, o, back=True).wait_recv()
            if g + ahead < len(order):
                piece(g + ahead, o).start()
        for m in range(4):
            r = pl.ds(base + m * width, width)
            if s:
                hi[r, at], lo[r, at] = halves(rx[m, STARTS[s] - 128:STARTS[s] - 128 + width, at])
            else:
                hi[r, at], lo[r, at] = (dot_nt(unit, half).astype(BF16) for half in halves(raw[m, at]))
        both = dot_nt(jnp.concatenate([hi[new, at], lo[new, at]], axis=0), hi[0:lanes, at])
        value = both[:count] + (both[count:] + dot_nt(hi[new, at], lo[0:lanes, at]))
        if k:
            acc[new, 0:lanes] += value
        else:
            acc[new, 0:lanes] = value
            if s and lanes < M:
                acc[new, lanes:M] = jnp.zeros((count, M - lanes), F32)
        if s == 0 and k + 1 < chunk // size:
            for o in range(4):
                transpose(o, k + 1)
        if (k + 1) * size == chunk:
            running.append(stage_sum(s))
        advance()
        if (s, k) == (2, 0):
            for w in sketch_waits:
                w.wait_recv()
            current = jnp.concatenate(
                [skb[m, :, r:r + w] for r, w in zip(STARTS, WIDTHS) for m in range(4)], axis=1)
            start[...] = jnp.concatenate([current, jnp.zeros((PAD - K, M), F32)], axis=0)
    for g in range(len(order)):
        for o in (1, 3, 2):
            piece(g, o).wait_send()
    while running:
        advance()
    keep(M - 128, 128, True)
    current = start[...]

    def image_of(value):
        return product(value, chi[...], clo[...], NN)

    def gram_of(image, value):
        top, low = halves(value)
        before, after = jnp.zeros((64, M), BF16), jnp.zeros((64 - PAD, M), BF16)
        return product(image, jnp.concatenate([before, top, after], axis=0),
                       jnp.concatenate([before, low, after], axis=0), NT)

    def apply(inverse, value):
        return product(inverse, *halves(value), NN)

    image = image_of(current)
    gram = gram_of(image, current)
    for turn_index in range(ITERS - 2):
        second = image_of(image)
        inverse = inverse_factor(gram)
        current = apply(inverse, image)
        image = apply(inverse, second)
        gram = gram_of(image, current)

    size = 512
    pieces = chunk // size
    parts = {}
    top, low = halves(image)
    stacked = jnp.concatenate([top, low], axis=0)
    dot_nn = functools.partial(lax.dot_general, dimension_numbers=NN, preferred_element_type=F32)
    for k in range(pieces):
        at = pl.ds(k * size, size)
        both = dot_nn(stacked, hi[:, at])
        yb[x, 0:K, at] = (both[:PAD] + (both[PAD:] + dot_nn(top, lo[:, at])))[:K]
        for o in (1, 3, 2):
            src = yb.at[x, pl.ds(0, K), at]
            parts[k, o] = copies.exchange(
                src, src, device(turn(x, o), y, z, core), yb.at[turn(x, 4 - o), pl.ds(0, K), at])
    second = image_of(image)
    inverse = inverse_factor(gram)
    current = apply(inverse, image)
    image = apply(inverse, second)
    last = inverse_factor(gram_of(image, current))
    current = apply(last, image)[:K]
    for m in range(4):
        natural[m] = jnp.concatenate(
            [current[:, 4 * r + m * w:4 * r + m * w + w] for r, w in zip(STARTS, WIDTHS)], axis=1)
    loadings[...] = natural[x]
    last = apply(last, inverse)
    for o in (0, 1, 3, 2):
        m = turn(x, 4 - o)
        for k in range(pieces):
            if o:
                parts[k, o].wait_recv()
            value = apply(last, yb[m, :, pl.ds(k * size, size)])
            basis[:, pl.ds(pl.multiple_of(m * chunk + k * size, size), size)] = value[:K]
    copies.finish()


def local(genotypes, sketch):
    chunk = genotypes.shape[0] // 4
    norm_scale = math.sqrt(genotypes.shape[0] * lax.axis_size("people"))
    n, pieces = len(WIDTHS), sum(chunk // size for size in PIECES)
    slots = n * (1 + 15 + 3 + 15 + 1) + 3 + 12
    vmem = pl.BlockSpec(memory_space=pltpu.VMEM)
    basis, loadings = pl.pallas_call(
        kernel,
        name="subspace_iteration",
        out_shape=(jax.ShapeDtypeStruct((K, genotypes.shape[0]), F32), jax.ShapeDtypeStruct((K, 256), F32)),
        in_specs=[pl.BlockSpec(memory_space=pl.ANY), vmem],
        out_specs=(vmem, vmem),
        scratch_shapes=[
            pltpu.VMEM((4, chunk, 128), F32),
            pltpu.VMEM((4, chunk, 128), F32),
            pltpu.VMEM((3, 128, chunk), F32),
            pltpu.VMEM((4, 128, chunk), F32),
            pltpu.VMEM((M, chunk), BF16),
            pltpu.VMEM((M, chunk), BF16),
            pltpu.VMEM((M, M), F32),
            pltpu.VMEM((M, M), F32),
            pltpu.VMEM((M, M), BF16),
            pltpu.VMEM((M, M), BF16),
            pltpu.VMEM((4, K, 256), F32),
            pltpu.VMEM((4, PAD, chunk), F32),
            pltpu.VMEM((M // 2, M), F32),
            pltpu.VMEM((M // 2, M), F32),
            pltpu.VMEM((15, M // 8, 256), F32),
            pltpu.VMEM((M // 8, 256), F32),
            pltpu.VMEM((4, M // 8, 256), F32),
            pltpu.VMEM((4, K, 256), F32),
            pltpu.VMEM((PAD, M), F32),
            pltpu.SemaphoreType.DMA((5,)),
            pltpu.SemaphoreType.DMA((pieces * 3,)),
            pltpu.SemaphoreType.DMA((pieces * 3,)),
            pltpu.SemaphoreType.DMA((slots,)),
            pltpu.SemaphoreType.DMA((slots,)),
        ],
        compiler_params=pltpu.CompilerParams(collective_id=0, has_side_effects=True, vmem_limit_bytes=62 << 20),
    )(genotypes, sketch)
    return basis * norm_scale, loadings / norm_scale


def solution(mesh):
    placed = (P("people", "markers"), P(None, "markers"))
    return jax.shard_map(
        local,
        mesh=mesh,
        in_specs=placed,
        out_specs=(P(None, "people"), P(None, "markers")),
        check_vma=False,
    )
```

```python
import functools
import math

import jax
import jax.numpy as jnp
from jax import lax
from jax.experimental import pallas as pl
from jax.experimental.pallas import tpu as pltpu
from jax.sharding import PartitionSpec as P

MESH = pl.DeviceIdType.MESH
ITERS = 5
M, K, PAD = 1024, 40, 48
WIDTHS = (128, 32, 32, 16, 16, 16, 16)
PIECES = (512, 512, 512, 1024, 1024, 1024, 512)
STARTS = tuple(sum(WIDTHS[:s]) for s in range(len(WIDTHS)))
PAUSES = ((1, 4, 5, 4, 1),) + ((1, 3, 4, 3, 1),) * 2 + ((1, 2, 3, 2, 1),) * 4
F32, BF16 = jnp.float32, jnp.bfloat16
NT = (((1,), (1,)), ((), ()))
NN = (((1,), (0,)), ((), ()))


def place():
    people, x = lax.axis_index("people"), lax.axis_index("markers")
    return x, people // 8, lax.rem(people // 2, 4), lax.rem(people, 2)


def device(x, y, z, core):
    return {"people": (y * 4 + z) * 2 + core, "markers": x}


def turn(index, step):
    return lax.rem(index + step, 4)


def halves(value):
    top = value.astype(BF16)
    return top, (value - top.astype(F32)).astype(BF16)


def product(left, right_top, right_low, dims):
    rows = left.shape[0]
    top, low = halves(left)
    dot = functools.partial(lax.dot_general, dimension_numbers=dims, preferred_element_type=F32)
    both = dot(jnp.concatenate([top, low], axis=0), right_top)
    return both[:rows] + (both[rows:] + dot(top, right_low))


def inverse_factor(work):
    lane = lax.broadcasted_iota(jnp.int32, (8, 128), 1)
    row = lax.broadcasted_iota(jnp.int32, (8, 128), 0)
    tiles = [work[8 * t:8 * t + 8] + jnp.where(lane == row + 8 * t, 1.0, 0.0) for t in range(K // 8)]
    for j in range(K):
        first, r = divmod(j, 8)
        pivot_row = tiles[first][r:r + 1]
        scaled = pivot_row / pivot_row[:, 64 + j:65 + j]
        for t in range(first, K // 8):
            column = jnp.broadcast_to(tiles[t][:, 64 + j:65 + j], (8, 128))
            if t == first:
                column = jnp.where(row > r, column, 0.0)
            tiles[t] = tiles[t] - column * scaled
    for t in range(K // 8):
        pivots = jnp.sum(jnp.where(lane == row + (64 + 8 * t), tiles[t], 0.0), axis=1, keepdims=True)
        tiles[t] = jnp.where(lane < K, tiles[t] / jnp.sqrt(pivots), 0.0)
    tiles += [jnp.zeros((8, 128), F32)] * ((PAD - K) // 8)
    return jnp.concatenate(tiles, axis=0)[:, :PAD]


class Copies:
    def __init__(self, send_sem, recv_sem, first):
        self.send_sem, self.recv_sem, self.count, self.open = send_sem, recv_sem, first, []

    def exchange(self, src, dst, to, landed):
        slot = self.count
        self.count += 1
        copy = pltpu.make_async_remote_copy(
            src_ref=src, dst_ref=dst, send_sem=self.send_sem.at[slot], recv_sem=self.recv_sem.at[slot],
            device_id=to, device_id_type=MESH)
        copy.start()
        self.open.append(copy)
        return pltpu.make_async_remote_copy(
            src_ref=landed, dst_ref=landed, send_sem=self.send_sem.at[slot], recv_sem=self.recv_sem.at[slot],
            device_id=to, device_id_type=MESH)

    def finish(self):
        for copy in self.open:
            copy.wait_send()
        self.open = []


def reduce_steps(base, count, span, pauses, copies, refs, here):
    acc, full, b1, s1, b2, s3, b4 = refs
    x, y, z, core = here
    half, part, wide = count // 2, count // 8, span // 4
    hb, pb = base // 2, base // 8
    lanes = pl.ds(0, span)
    mine = pl.ds(pl.multiple_of(base + core * half, 8), half)
    other = pl.ds(pl.multiple_of(base + (1 - core) * half, 8), half)
    h = pl.ds(hb, half)
    p = (pl.ds(pb, part), pl.ds(0, wide))
    plane = [(i, j) for i in range(4) for j in range(4) if i or j]
    got = copies.exchange(acc.at[other, lanes], b1.at[h, lanes], device(x, y, z, 1 - core), b1.at[h, lanes])
    yield from (None,) * pauses[0]
    got.wait_recv()
    s1[h, lanes] = acc[mine, lanes] + b1[h, lanes]

    def cut(row, lane, offset):
        return (pl.ds(pl.multiple_of(offset + row * part, 8), part), pl.ds(pl.multiple_of(lane * wide, 128), wide))

    waits = []
    for n, (i, j) in enumerate(plane):
        waits.append(copies.exchange(
            s1.at[cut(turn(y, i), turn(z, j), hb)], b2.at[(n,) + p],
            device(x, turn(y, i), turn(z, j), core), b2.at[(n,) + p]))
    yield from (None,) * pauses[1]
    for w in waits:
        w.wait_recv()
    total = s1[cut(y, z, hb)]
    for n in range(len(plane)):
        total = total + b2[(n,) + p]
    s3[p] = total
    b4[(x,) + p] = total
    waits = []
    for o in (2, 1, 3):
        waits.append(copies.exchange(
            s3.at[p], b4.at[(x,) + p], device(turn(x, o), y, z, core), b4.at[(turn(x, 4 - o),) + p]))
    yield from (None,) * pauses[2]
    for w in waits:
        w.wait_recv()
    offset = base + core * half
    at = full.at[cut(y, z, offset)]
    full[cut(y, z, offset)] = (b4[(0,) + p] + b4[(1,) + p]) + (b4[(2,) + p] + b4[(3,) + p])
    waits = []
    for i, j in plane:
        waits.append(copies.exchange(
            at, at, device(x, turn(y, i), turn(z, j), core), full.at[cut(turn(y, 4 - i), turn(z, 4 - j), offset)]))
    yield from (None,) * pauses[3]
    for w in waits:
        w.wait_recv()
    at = full.at[mine, lanes]
    got = copies.exchange(at, at, device(x, y, z, 1 - core), full.at[other, lanes])
    yield from (None,) * pauses[4]
    got.wait_recv()


def kernel(a, sketch, basis, loadings, raw, staged, turned, rx, hi, lo, acc, full, chi, clo, skb, yb, b1, s1, b2, s3,
           b4, natural, start, load_sem, piece_send, piece_recv, send_sem, recv_sem):
    here = x, y, z, core = place()
    chunk = a.shape[0] // 4
    own = pl.ds(pl.multiple_of(x * chunk, chunk), chunk)
    first_half, second_half = pl.ds(0, 128), pl.ds(128, 128)
    own_raw = pltpu.make_async_copy(a.at[own, first_half], raw.at[x], load_sem.at[0])
    own_raw.start()
    barrier = pltpu.get_barrier_semaphore()
    partners = [device(x, y, z, 1 - core)]
    partners += [device(turn(x, o), y, z, core) for o in (1, 2, 3)]
    partners += [device(x, turn(y, i), turn(z, j), core) for i in range(4) for j in range(4) if i or j]
    for partner in partners:
        pl.semaphore_signal(barrier, inc=1, device_id=partner, device_id_type=MESH)
    copies = Copies(send_sem, recv_sem, 40 * len(WIDTHS))
    order = [(s, k) for s in range(len(WIDTHS)) for k in range(chunk // PIECES[s])]

    def piece(g, o, back=False):
        s, k = order[g]
        at = pl.ds(k * PIECES[s], PIECES[s])
        sems = dict(send_sem=piece_send.at[g * 3 + o - 1], recv_sem=piece_recv.at[g * 3 + o - 1],
                    device_id=device(turn(x, o), y, z, core), device_id_type=MESH)
        if s == 0:
            src = a.at[pl.ds(pl.multiple_of(turn(x, o) * chunk + k * PIECES[s], PIECES[s]), PIECES[s]), first_half]
            spot = (at,)
            into = raw
        else:
            r = pl.ds(STARTS[s] - 128, WIDTHS[s])
            src = turned.at[o - 1, r, at]
            spot = (r, at)
            into = rx
        if back:
            landed = into.at[(turn(x, 4 - o),) + spot]
            return pltpu.make_async_remote_copy(src_ref=landed, dst_ref=landed, **sems)
        return pltpu.make_async_remote_copy(src_ref=src, dst_ref=into.at[(x,) + spot], **sems)

    ahead = 2
    pl.semaphore_wait(barrier, len(partners))
    for g in range(ahead):
        for o in (1, 3, 2):
            piece(g, o).start()
    skb[x] = sketch[...]
    sketch_waits = [
        copies.exchange(sketch, skb.at[x], device(turn(x, o), y, z, core), skb.at[turn(x, 4 - o)]) for o in (1, 2, 3)]
    loads = {}
    for o in range(4):
        load = pltpu.make_async_copy(
            a.at[pl.ds(pl.multiple_of(turn(x, o) * chunk, chunk), chunk), second_half], staged.at[o], load_sem.at[o + 1])
        load.start()
        loads[o] = load
    yb[:, K:PAD] = jnp.zeros((4, PAD - K, chunk), F32)

    def transpose(o, k):
        at = pl.ds(k * PIECES[0], PIECES[0])
        block = staged[o, at].T
        if o:
            turned[o - 1, :, at] = block
        else:
            rx[x, :, at] = block

    for o in range(4):
        loads[o].wait()
        transpose(o, 0)
    own_raw.wait()

    refs = (acc, full, b1, s1, b2, s3, b4)
    running, tail, unfinished = [], [], []

    def keep(base, count, halved=False):
        value = full[base:base + count, 0:base + count]
        block = value[:, base:base + count]
        if halved:
            r = lax.broadcasted_iota(jnp.int32, (count, count), 0)
            c = lax.broadcasted_iota(jnp.int32, (count, count), 1)
            block = jnp.where((r < count // 2) & (c >= count // 2), block.T, block)
        chi[base:base + count, base:base + count], clo[base:base + count, base:base + count] = halves(block)
        if base:
            side = value[:, 0:base]
            chi[base:base + count, 0:base], clo[base:base + count, 0:base] = halves(side)
            chi[0:base, base:base + count], clo[0:base, base:base + count] = halves(side.T)

    def stage_sum(s):
        base, count = 4 * STARTS[s], 4 * WIDTHS[s]
        mine = Copies(send_sem, recv_sem, 40 * s)
        yield from reduce_steps(base, count, M if s else count, PAUSES[s], mine, refs, here)
        if tail:
            unfinished.append(mine)
        else:
            mine.finish()
        if WIDTHS[s] > 16:
            keep(base, count)
        elif s % 2 == 0 and base + count < M:
            keep(base - count, 2 * count, True)

    def advance():
        for item in reversed(list(running)):
            try:
                next(item)
            except StopIteration:
                running.remove(item)

    dot_nt = functools.partial(lax.dot_general, dimension_numbers=NT, preferred_element_type=F32)
    unit = jnp.where(lax.broadcasted_iota(jnp.int32, (128, 128), 0) == lax.broadcasted_iota(jnp.int32, (128, 128), 1),
                     1.0, 0.0).astype(BF16)
    for g, (s, k) in enumerate(order):
        width, size = WIDTHS[s], PIECES[s]
        base, count = 4 * STARTS[s], 4 * width
        lanes = base + count
        at = pl.ds(k * size, size)
        new = pl.ds(base, count)
        for o in (1, 3, 2):
            piece(g, o, back=True).wait_recv()
            piece(g, o).wait_send()
            if g + ahead < len(order):
                piece(g + ahead, o).start()
        for m in range(4):
            r = pl.ds(base + m * width, width)
            if s:
                hi[r, at], lo[r, at] = halves(rx[m, STARTS[s] - 128:STARTS[s] - 128 + width, at])
            else:
                hi[r, at], lo[r, at] = (dot_nt(unit, half).astype(BF16) for half in halves(raw[m, at]))
        both = dot_nt(jnp.concatenate([hi[new, at], lo[new, at]], axis=0), hi[0:lanes, at])
        value = both[:count] + (both[count:] + dot_nt(hi[new, at], lo[0:lanes, at]))
        if k:
            acc[new, 0:lanes] += value
        else:
            acc[new, 0:lanes] = value
            if s and lanes < M:
                acc[new, lanes:M] = jnp.zeros((count, M - lanes), F32)
        if s == 0 and k + 1 < chunk // size:
            for o in range(4):
                transpose(o, k + 1)
        if (k + 1) * size == chunk:
            running.append(stage_sum(s))
        advance()
        if (s, k) == (2, 0):
            for w in sketch_waits:
                w.wait_recv()
            current = jnp.concatenate(
                [skb[m, :, r:r + w] for r, w in zip(STARTS, WIDTHS) for m in range(4)], axis=1)
            start[...] = jnp.concatenate([current, jnp.zeros((PAD - K, M), F32)], axis=0)
    tail.append(True)
    while running:
        advance()
    keep(M - 128, 128, True)
    current = start[...]

    def image_of(value):
        return product(value, chi[...], clo[...], NN)

    def gram_of(image, value):
        top, low = halves(value)
        before, after = jnp.zeros((64, M), BF16), jnp.zeros((64 - PAD, M), BF16)
        return product(image, jnp.concatenate([before, top, after], axis=0),
                       jnp.concatenate([before, low, after], axis=0), NT)

    def apply(inverse, value):
        return product(inverse, *halves(value), NN)

    image = image_of(current)
    gram = gram_of(image, current)
    for turn_index in range(ITERS - 2):
        second = image_of(image)
        inverse = inverse_factor(gram)
        current = apply(inverse, image)
        image = apply(inverse, second)
        gram = gram_of(image, current)

    size = 512
    pieces = chunk // size
    parts = {}
    top, low = halves(image)
    stacked = jnp.concatenate([top, low], axis=0)
    dot_nn = functools.partial(lax.dot_general, dimension_numbers=NN, preferred_element_type=F32)
    for k in range(pieces):
        at = pl.ds(k * size, size)
        both = dot_nn(stacked, hi[:, at])
        yb[x, 0:K, at] = (both[:PAD] + (both[PAD:] + dot_nn(top, lo[:, at])))[:K]
        for o in (1, 3, 2):
            src = yb.at[x, pl.ds(0, K), at]
            parts[k, o] = copies.exchange(
                src, src, device(turn(x, o), y, z, core), yb.at[turn(x, 4 - o), pl.ds(0, K), at])
    second = image_of(image)
    inverse = inverse_factor(gram)
    current = apply(inverse, image)
    image = apply(inverse, second)
    last = inverse_factor(gram_of(image, current))
    current = apply(last, image)[:K]
    for m in range(4):
        natural[m] = jnp.concatenate(
            [current[:, 4 * r + m * w:4 * r + m * w + w] for r, w in zip(STARTS, WIDTHS)], axis=1)
    loadings[...] = natural[x]
    last = apply(last, inverse)
    for item in unfinished:
        item.finish()
    for o in (0, 1, 3, 2):
        m = turn(x, 4 - o)
        for k in range(pieces):
            if o:
                parts[k, o].wait_recv()
            value = apply(last, yb[m, :, pl.ds(k * size, size)])
            basis[:, pl.ds(pl.multiple_of(m * chunk + k * size, size), size)] = value[:K]
    copies.finish()


def local(genotypes, sketch):
    chunk = genotypes.shape[0] // 4
    norm_scale = math.sqrt(genotypes.shape[0] * lax.axis_size("people"))
    n, pieces = len(WIDTHS), sum(chunk // size for size in PIECES)
    slots = 40 * n + 3 + 12
    vmem = pl.BlockSpec(memory_space=pltpu.VMEM)
    basis, loadings = pl.pallas_call(
        kernel,
        name="subspace_iteration",
        out_shape=(jax.ShapeDtypeStruct((K, genotypes.shape[0]), F32), jax.ShapeDtypeStruct((K, 256), F32)),
        in_specs=[pl.BlockSpec(memory_space=pl.ANY), vmem],
        out_specs=(vmem, vmem),
        scratch_shapes=[
            pltpu.VMEM((4, chunk, 128), F32),
            pltpu.VMEM((4, chunk, 128), F32),
            pltpu.VMEM((3, 128, chunk), F32),
            pltpu.VMEM((4, 128, chunk), F32),
            pltpu.VMEM((M, chunk), BF16),
            pltpu.VMEM((M, chunk), BF16),
            pltpu.VMEM((M, M), F32),
            pltpu.VMEM((M, M), F32),
            pltpu.VMEM((M, M), BF16),
            pltpu.VMEM((M, M), BF16),
            pltpu.VMEM((4, K, 256), F32),
            pltpu.VMEM((4, PAD, chunk), F32),
            pltpu.VMEM((M // 2, M), F32),
            pltpu.VMEM((M // 2, M), F32),
            pltpu.VMEM((15, M // 8, 256), F32),
            pltpu.VMEM((M // 8, 256), F32),
            pltpu.VMEM((4, M // 8, 256), F32),
            pltpu.VMEM((4, K, 256), F32),
            pltpu.VMEM((PAD, M), F32),
            pltpu.SemaphoreType.DMA((5,)),
            pltpu.SemaphoreType.DMA((pieces * 3,)),
            pltpu.SemaphoreType.DMA((pieces * 3,)),
            pltpu.SemaphoreType.DMA((slots,)),
            pltpu.SemaphoreType.DMA((slots,)),
        ],
        compiler_params=pltpu.CompilerParams(collective_id=0, has_side_effects=True, vmem_limit_bytes=62 << 20),
    )(genotypes, sketch)
    return basis * norm_scale, loadings / norm_scale


def solution(mesh):
    placed = (P("people", "markers"), P(None, "markers"))
    return jax.shard_map(
        local,
        mesh=mesh,
        in_specs=placed,
        out_specs=(P(None, "people"), P(None, "markers")),
        check_vma=False,
    )
```
